32 devices in a mesh: wide: 8 (over z, x), narrow: 4 (over y, core).
Axes of the slice: x: 2, y: 2, z: 4, core: 2. Of those that a mesh axis runs over, the one named last changes fastest.
Arguments:
- tokens: bfloat16 [36864, 768], P(('wide', 'narrow')), may hold values from -6 to 6
- ln1_gain: bfloat16 [768], replicated, may hold values from 0.25 to 1.75
- ln1_bias: bfloat16 [768], replicated, may hold values from -4 to 4
- w_qkv: bfloat16 [768, 2304], replicated, may hold values from -0.21875 to 0.21875
- b_qkv: bfloat16 [2304], replicated, may hold values from -4 to 4
- qnorm_gain: bfloat16 [64], replicated, may hold values from 0.25 to 1.75
- qnorm_bias: bfloat16 [64], replicated, may hold values from -4 to 4
- knorm_gain: bfloat16 [64], replicated, may hold values from 0.25 to 1.75
- w_out: bfloat16 [768, 768], replicated, may hold values from -0.875 to 0.875
- b_out: bfloat16 [768], replicated, may hold values from -4 to 4
- ln2_gain: bfloat16 [768], replicated, may hold values from 0.25 to 1.75
- ln2_bias: bfloat16 [768], replicated, may hold values from -4 to 4
- w_up: bfloat16 [768, 3072], replicated, may hold values from -0.21875 to 0.21875
- b_up: bfloat16 [3072], replicated, may hold values from -4 to 4
- w_down: bfloat16 [3072, 768], replicated, may hold values from -0.109375 to 0.109375
- b_down: bfloat16 [768], replicated, may hold values from -4 to 4
- segment_ids: int32 [36864], P(('wide', 'narrow')), may hold values from -1 to 15, as said below
- bucket_ids: int32 [8], P('wide'), may hold values from 0 to 1, as said below
- share_counts: int32 [2], replicated, may hold values from 1000 to 99999
- cotangent: bfloat16 [36864, 768], P(('wide', 'narrow')), may hold values from -6 to 6
Outputs:
- out_tokens: bfloat16 [36864, 768], P(('wide', 'narrow'))
- grad_tokens: bfloat16 [36864, 768], P(('wide', 'narrow'))
- grad_ln1_gain: float32 [768], replicated
- grad_ln1_bias: float32 [768], replicated
- grad_w_qkv: float32 [768, 2304], replicated
- grad_b_qkv: float32 [2304], replicated
- grad_qnorm_gain: float32 [64], replicated
- grad_qnorm_bias: float32 [64], replicated
- grad_knorm_gain: float32 [64], replicated
- grad_w_out: float32 [768, 768], replicated
- grad_b_out: float32 [768], replicated
- grad_ln2_gain: float32 [768], replicated
- grad_ln2_bias: float32 [768], replicated
- grad_w_up: float32 [768, 3072], replicated
- grad_b_up: float32 [3072], replicated
- grad_w_down: float32 [3072, 768], replicated
- grad_b_down: float32 [768], replicated
The draws below stay inside these ranges and needn't reach their ends.
Inputs may be any that keep to these rules, and one draw needn't show every extreme that they name: bucket_ids is 1 on the indices of wide below a split and 0 on the rest; both buckets are present. `segment_ids`: within a device's block of 1152 slots, a large-bucket block holds 2 image slots of 576, a small-bucket block slots of 64; slot j's patches come first in it and carry the number j, the rest of the slot is -1; slot 0 is always full; in a small-bucket block the last eighth of the slots is empty.
All inputs are finite; a program needn't handle non-finite values.
Results may differ from the reference program's by a relative error of at most 0.012.
Values sent between devices are 32-bit elements; how exact they have to be, the bound alone decides.
A program may use at most 384 MiB of HBM per device.

```python
import jax
import jax.numpy as jnp
from jax import lax

D = 768
HEAD_DIM = 64
FF = 3072
LARGE_IMG = 576
SMALL_IMG = 64
TOK_DEV = 1152
TOKENS = 36864
N_WIDE = 8
N_NARROW = 4


def split_point(key):
    return jax.random.randint(key, (), 1, N_WIDE)


def draw_bucket_ids(key, part):
    split = split_point(key)
    return jnp.where(jnp.arange(N_WIDE) < split, 1, 0).astype(jnp.int32)


def draw_segment_ids(key, part):
    split = split_point(key)
    key = jax.random.fold_in(key, 5)
    devices = TOKENS // TOK_DEV
    bucket = jnp.where(jnp.arange(devices) // N_NARROW < split, 1, 0)
    key_large, key_small = jax.random.split(key)
    large_slots = TOK_DEV // LARGE_IMG
    large_len = jax.random.randint(key_large, (devices, large_slots), LARGE_IMG // 2, LARGE_IMG + 1)
    large_len = large_len.at[:, 0].set(LARGE_IMG)
    small_slots = TOK_DEV // SMALL_IMG
    small_len = jax.random.randint(key_small, (devices, small_slots), max(1, SMALL_IMG // 4), SMALL_IMG + 1)
    small_len = small_len.at[:, 0].set(SMALL_IMG)
    empty = small_slots // 8
    small_len = jnp.where(jnp.arange(small_slots)[None, :] >= small_slots - empty, 0, small_len)
    position = jnp.arange(TOK_DEV)
    large_slot = position // LARGE_IMG
    large_live = (position % LARGE_IMG)[None, :] < large_len[:, large_slot]
    large_seg = jnp.where(large_live, large_slot[None, :], -1)
    small_slot = position // SMALL_IMG
    small_live = (position % SMALL_IMG)[None, :] < small_len[:, small_slot]
    small_seg = jnp.where(small_live, small_slot[None, :], -1)
    segments = jnp.where(bucket[:, None] == 1, large_seg, small_seg)
    return segments.reshape(TOKENS).astype(jnp.int32)


def steps_of(rng, dims, cuts, low, top_value):
    gain = 1.0
    for axis_at, parts in cuts:
        draws = jax.random.uniform(jax.random.fold_in(jax.random.fold_in(rng, 6), axis_at), (parts,), jnp.float32, low / len(cuts), top_value / len(cuts))
        gain = gain * jnp.repeat(jnp.exp(draws), dims[axis_at] // parts).reshape((-1,) + (1,) * (len(dims) - 1 - axis_at))
    return gain


def gaussian(stream_key, dims, deviation, bound, cuts=(), dtype=jnp.bfloat16):
    gain = steps_of(stream_key, dims, cuts, -0.22, 0.18) if cuts else 1.0
    drawn = jax.random.normal(stream_key, dims, jnp.float32) * deviation * gain
    return jnp.minimum(jnp.maximum(drawn, -bound), bound).astype(dtype)


def setup_inputs(seed: int = 0) -> dict:
    seeds = jax.random.split(jax.random.key(seed), 21)
    tokens = gaussian(seeds[0], (TOKENS, D), 1.0, 6.0, ((0, 32),))
    ln1_gain = jnp.clip(1.0 + 0.15 * jax.random.normal(seeds[1], (D,), jnp.float32), 0.25, 1.75).astype(jnp.bfloat16)
    ln1_bias = gaussian(seeds[2], (D,), 0.3, 4.0)
    w_qkv = gaussian(seeds[3], (D, 3 * D), D ** -0.5, 0.21875)
    b_qkv = gaussian(seeds[4], (3 * D,), 0.3, 4.0)
    qnorm_gain = jnp.clip(1.0 + 0.15 * jax.random.normal(seeds[5], (HEAD_DIM,), jnp.float32), 0.25, 1.75).astype(jnp.bfloat16)
    qnorm_bias = gaussian(seeds[6], (HEAD_DIM,), 0.3, 4.0)
    knorm_gain = jnp.clip(1.0 + 0.15 * jax.random.normal(seeds[7], (HEAD_DIM,), jnp.float32), 0.25, 1.75).astype(jnp.bfloat16)
    w_out = gaussian(seeds[8], (D, D), (D // 16) ** -0.5, 0.875)
    b_out = gaussian(seeds[9], (D,), 0.3, 4.0)
    ln2_gain = jnp.clip(1.0 + 0.15 * jax.random.normal(seeds[10], (D,), jnp.float32), 0.25, 1.75).astype(jnp.bfloat16)
    ln2_bias = gaussian(seeds[11], (D,), 0.3, 4.0)
    w_up = gaussian(seeds[12], (D, FF), D ** -0.5, 0.21875)
    b_up = gaussian(seeds[13], (FF,), 0.3, 4.0)
    w_down = gaussian(seeds[14], (FF, D), FF ** -0.5, 0.109375)
    b_down = gaussian(seeds[15], (D,), 0.3, 4.0)
    segment_ids = draw_segment_ids(jax.random.fold_in(seeds[20], 71), 0)
    bucket_ids = draw_bucket_ids(jax.random.fold_in(seeds[20], 71), 0)
    share_counts = jax.random.randint(seeds[18], (2,), 1000, 100000).astype(jnp.int32)
    cotangent = gaussian(seeds[19], (TOKENS, D), 1.0, 6.0, ((0, 32),))
    return {"tokens": tokens, "ln1_gain": ln1_gain, "ln1_bias": ln1_bias, "w_qkv": w_qkv, "b_qkv": b_qkv, "qnorm_gain": qnorm_gain, "qnorm_bias": qnorm_bias, "knorm_gain": knorm_gain, "w_out": w_out, "b_out": b_out, "ln2_gain": ln2_gain, "ln2_bias": ln2_bias, "w_up": w_up, "b_up": b_up, "w_down": w_down, "b_down": b_down, "segment_ids": segment_ids, "bucket_ids": bucket_ids, "share_counts": share_counts, "cotangent": cotangent}


EPS = 1e-06
HIGH = lax.Precision.HIGHEST

@jax.custom_vjp
def low(v):
    return lax.optimization_barrier(v.astype(jnp.bfloat16)).astype(jnp.float32)

@jax.custom_vjp
def low_back(v):
    return v

def low_keep(v):
    return (low(v), None)

def low_pass(kept, grad):
    return (grad,)

def back_keep(v):
    return (v, None)

def back_low(kept, grad):
    return (low(grad),)
low.defvjp(low_keep, low_pass)
low_back.defvjp(back_keep, back_low)

def norm_rows(v):
    centred = v - lax.optimization_barrier(jnp.mean(v, axis=-1, keepdims=True))
    return centred * lax.rsqrt(lax.optimization_barrier(jnp.mean(centred * centred, axis=-1, keepdims=True)) + EPS)

def matmul(left, right):
    return jnp.dot(left, right, precision=HIGH, preferred_element_type=jnp.float32)

def layer(inputs, params, segments):
    g_one, b_one, w_qkv, b_qkv, q_gain, q_bias, k_gain, w_out, b_out, g_two, b_two, w_up, b_up, w_down, b_down = params
    rows, width = inputs.shape
    head_dim = q_gain.shape[0]
    heads = width // head_dim
    scale = head_dim ** (-0.5)
    hidden1 = low(norm_rows(inputs) * g_one + b_one)
    project = low_back(matmul(hidden1, w_qkv) + b_qkv)
    queries = project[:, :width].reshape(rows, heads, head_dim)
    keys = project[:, width:2 * width].reshape(rows, heads, head_dim)
    values = project[:, 2 * width:].reshape(rows, heads, head_dim)
    qnormed = low(norm_rows(queries) * q_gain + q_bias)
    knormed = low(norm_rows(keys) * k_gain)
    vrounded = low(values)
    blocks = max(1, rows // 512)
    block_rows = rows // blocks
    q_blocks = qnormed.reshape(blocks, block_rows, heads, head_dim)
    seg_blocks = segments.reshape(blocks, block_rows)

    def attend(pieces):
        q_part, seg_part = pieces
        scores = jnp.einsum('qhd,khd->hqk', q_part, knormed, precision=HIGH) * scale
        same = seg_part[:, None] == segments[None, :]
        scores = low_back(jnp.where(same[None], scores, -1000000000.0))
        top = lax.optimization_barrier(jnp.max(scores, axis=-1, keepdims=True))
        expo = jnp.exp(scores - top)
        probs = expo / lax.optimization_barrier(jnp.sum(expo, axis=-1, keepdims=True))
        return jnp.einsum('hqk,khd->qhd', low(probs), vrounded, precision=HIGH)
    attended = lax.map(jax.checkpoint(attend), (q_blocks, seg_blocks)).reshape(rows, width)
    attended = low(low_back(attended))
    branch = low_back(matmul(attended, w_out) + b_out)
    resid = inputs + branch
    hidden2 = low(norm_rows(resid) * g_two + b_two)
    upper = low_back(matmul(hidden2, w_up) + b_up)
    act = low(jax.nn.gelu(upper, approximate=False))
    mlp = low_back(matmul(act, w_down) + b_down)
    return resid + mlp

def reference(tokens, ln1_gain, ln1_bias, w_qkv, b_qkv, qnorm_gain, qnorm_bias, knorm_gain, w_out, b_out, ln2_gain, ln2_bias, w_up, b_up, w_down, b_down, segment_ids, bucket_ids, share_counts, cotangent):
    params = tuple((p.astype(jnp.float32) for p in (ln1_gain, ln1_bias, w_qkv, b_qkv, qnorm_gain, qnorm_bias, knorm_gain, w_out, b_out, ln2_gain, ln2_bias, w_up, b_up, w_down, b_down)))
    devices = TOKENS // TOK_DEV
    width = tokens.shape[1]
    tok_blocks = tokens.astype(jnp.float32).reshape(devices, TOK_DEV, width)
    cot_blocks = cotangent.astype(jnp.float32).reshape(devices, TOK_DEV, width)
    seg_blocks = segment_ids.reshape(devices, TOK_DEV)
    dev_bucket = jnp.repeat(bucket_ids, N_NARROW)
    counts = share_counts.astype(jnp.float32)
    shares = counts / jnp.sum(counts)
    norm_factor = lax.rsqrt(jnp.float32(TOKENS))

    def one_block(totals, pieces):
        inputs, seg, cot, bucket = pieces
        out, pullback = jax.vjp(lambda v, *p: layer(v, p, seg), inputs, *params)
        live = (seg >= 0).astype(jnp.float32)
        grads = pullback(cot * live[:, None])
        share = jnp.sum(jnp.where(jnp.arange(2) == bucket, shares, 0.0))
        factor = share * norm_factor
        totals = tuple((t + factor * g for t, g in zip(totals, grads[1:])))
        return (totals, (out.astype(jnp.bfloat16), grads[0].astype(jnp.bfloat16)))
    zeros = tuple((jnp.zeros_like(p) for p in params))
    totals, (outs, grad_in) = lax.scan(one_block, zeros, (tok_blocks, seg_blocks, cot_blocks, dev_bucket))
    out_tokens = outs.reshape(TOKENS, width)
    grad_tokens = grad_in.reshape(TOKENS, width)
    return (out_tokens, grad_tokens, totals[0], totals[1], totals[2], totals[3], totals[4], totals[5], totals[6], totals[7], totals[8], totals[9], totals[10], totals[11], totals[12], totals[13], totals[14])
```

```python
import functools
import math

import jax
import jax.numpy as jnp
from jax import lax
from jax.experimental import pallas as pl
from jax.experimental.pallas import tpu as pltpu
from jax.sharding import PartitionSpec as P

EPS = 1e-06
F32 = jnp.float32
BF16 = jnp.bfloat16
NN = (((1,), (0,)), ((), ()))
NT = (((1,), (1,)), ((), ()))
MASKED = -1000000000.0
OPEN = 3.0e38
GROUP = 256
VMEM = 60 * 1024 * 1024


def dot(left, right, dims=NN):
    return lax.dot_general(left, right, dims, preferred_element_type=F32)


def row_stats(v):
    mean = jnp.mean(v, axis=-1, keepdims=True)
    centred = v - mean
    rstd = lax.rsqrt(jnp.mean(centred * centred, axis=-1, keepdims=True) + EPS)
    return centred * rstd, rstd


def head_mean(v, averager):
    high = v.astype(BF16)
    low = (v - high.astype(F32)).astype(BF16)
    return dot(high, averager) + dot(low, averager)


def averager_of(width, head_dim):
    row = lax.broadcasted_iota(jnp.int32, (width, width), 0) // head_dim
    col = lax.broadcasted_iota(jnp.int32, (width, width), 1) // head_dim
    return jnp.where(row == col, 1.0 / head_dim, 0.0).astype(BF16)


def row_loop(rows, chunk, body):
    def step(i, carry):
        body(pl.ds(pl.multiple_of(i * chunk, chunk), chunk))
        return carry

    lax.fori_loop(0, rows // chunk, step, 0)


def forward_kernel(
    head_dim,
    blocks,
    bucket_ref,
    x_ref,
    g1_ref,
    b1_ref,
    wq_ref,
    wk_ref,
    wv_ref,
    bq_ref,
    bk_ref,
    bv_ref,
    qg_ref,
    qb_ref,
    kg_ref,
    wo_ref,
    bo_ref,
    g2_ref,
    b2_ref,
    segc_ref,
    segr_ref,
    h1_ref,
    qn_ref,
    kn_ref,
    v_ref,
    qhat_ref,
    khat_ref,
    qrstd_ref,
    krstd_ref,
    lse_ref,
    ot_ref,
    r_ref,
    h2_ref,
    mask_s,
    vt_s,
    ot_s,
    o_s,
):
    rows, width = x_ref.shape
    group = wq_ref.shape[1]
    heads = group // head_dim
    span = rows // blocks
    chunk = span // 2
    step = pl.program_id(0)
    last = pl.num_programs(0) - 1
    scale = head_dim**-0.5

    @pl.when(step == 0)
    def _():
        def norm(at):
            hat, _ = row_stats(x_ref[at, :].astype(F32))
            h1_ref[at, :] = (hat * g1_ref[...] + b1_ref[...]).astype(BF16)

        row_loop(rows, span // 4, norm)
        for kb in range(blocks):
            for qb in range(blocks):
                same = segc_ref[kb * span : (kb + 1) * span, :] == segr_ref[qb]
                mask_s[kb, qb] = jnp.where(same, OPEN, MASKED)

    averager = averager_of(group, head_dim)

    def project(at):
        h1 = h1_ref[at, :]

        def normed(w_ref, bias_ref, hat_ref, rstd_ref):
            raw = dot(h1, w_ref[...]) + bias_ref[...]
            centred = raw - head_mean(raw, averager)
            rstd = lax.rsqrt(head_mean(centred * centred, averager) + EPS)
            hat = centred * rstd
            hat_ref[at, :] = hat
            rstd_ref[at, :] = rstd
            return hat

        qhat = normed(wq_ref, bq_ref, qhat_ref, qrstd_ref)
        qn_ref[at, :] = (qhat * qg_ref[...] + qb_ref[...]).astype(BF16)
        khat = normed(wk_ref, bk_ref, khat_ref, krstd_ref)
        kn_ref[at, :] = (khat * kg_ref[...]).astype(BF16)
        v_ref[at, :] = (dot(h1, wv_ref[...]) + bv_ref[...]).astype(BF16)

    row_loop(rows, chunk, project)
    for b in range(blocks):
        vt_s[b] = v_ref[b * span : (b + 1) * span, :].astype(F32).T.astype(BF16)

    lane_head = lax.broadcasted_iota(jnp.int32, (span, group), 1) // head_dim

    def attend(i, key_blocks):
        h = i // blocks
        qb = i % blocks
        queries = qn_ref[pl.ds(pl.multiple_of(qb * span, span), span), :]
        scores = []
        for kb in key_blocks(qb):
            keys = kn_ref[pl.ds(pl.multiple_of(kb * span, span), span), :] * jnp.asarray(scale, BF16)
            keys = jnp.where(lane_head == h, keys, jnp.zeros_like(keys))
            scores.append(jnp.minimum(dot(keys, queries, NT), mask_s[kb, qb]))
        top = functools.reduce(jnp.maximum, [jnp.max(s, axis=0, keepdims=True) for s in scores])
        expos = [jnp.exp(s - top) for s in scores]
        total = sum(jnp.sum(e, axis=0, keepdims=True) for e in expos)
        at = pl.ds(pl.multiple_of(h * head_dim, head_dim), head_dim)
        out = sum(
            dot(vt_s[kb, at, :], e.astype(BF16)) for kb, e in zip(key_blocks(qb), expos)
        )
        ot_s[qb, at, :] = out * (1.0 / total)
        lse_ref[h, qb] = top + jnp.log(total)

    large = bucket_ref[0] == 1

    @pl.when(large)
    def _():
        lax.fori_loop(
            0, heads * blocks, lambda i, c: (attend(i, lambda qb: [qb]), c)[1], 0
        )

    @pl.when(jnp.logical_not(large))
    def _():
        lax.fori_loop(
            0, heads * blocks, lambda i, c: (attend(i, lambda qb: list(range(blocks))), c)[1], 0
        )

    for b in range(blocks):
        piece = ot_s[b]
        ot_ref[b] = piece.astype(BF16)
        o_s[b * span : (b + 1) * span, :] = piece.T.astype(BF16)

    def out_project(at):
        part = dot(o_s[at, :], wo_ref[...])

        @pl.when(step == 0)
        def _():
            r_ref[at, :] = x_ref[at, :].astype(F32) + bo_ref[...] + part

        @pl.when(step > 0)
        def _():
            r_ref[at, :] += part

        @pl.when(step == last)
        def _():
            hat, _ = row_stats(r_ref[at, :])
            h2_ref[at, :] = (hat * g2_ref[...] + b2_ref[...]).astype(BF16)

    row_loop(rows, chunk, out_project)


def gelu_parts(u):
    size = jnp.abs(u) * (2.0**-0.5)
    below = 1.0 + 0.3275911 * size
    t = pl.reciprocal(below, approx=True)
    t = t * (2.0 - below * t)
    bell = jnp.exp(-0.5 * u * u)
    poly = t * (
        0.127414796
        + t * (-0.142248368 + t * (0.7107068705 + t * (-0.7265760135 + t * 0.5307027145)))
    )
    tail = poly * bell
    phi = jnp.where(u < 0.0, tail, 1.0 - tail)
    return phi, bell * (1.0 / math.sqrt(2.0 * math.pi))


def mlp_kernel(
    blocks,
    factor_ref,
    h2_ref,
    r_ref,
    cot_ref,
    live_ref,
    wu_ref,
    bu_ref,
    wd_ref,
    bd_ref,
    g2_ref,
    wo_ref,
    ot_ref,
    out_ref,
    gr_ref,
    go_ref,
    dwd_ref,
    dwu_ref,
    dwo_ref,
    dbu_ref,
    small_ref,
    gm_s,
    h2t_s,
    a_s,
    gu_s,
    m_s,
    gh2_s,
):
    rows, width = h2_ref.shape
    span = rows // blocks
    chunk = span // 2
    step = pl.program_id(0)
    last = pl.num_programs(0) - 1
    factor = factor_ref[0]

    @pl.when(step == 0)
    def _():
        small_ref[...] = jnp.zeros_like(small_ref)

        def start(at):
            gm = cot_ref[at, :].astype(F32) * live_ref[at, :]
            gm_s[at, :] = gm.astype(BF16)
            small_ref[0:1, :] += factor * jnp.sum(gm, axis=0, keepdims=True)
            m_s[at, :] = r_ref[at, :] + bd_ref[...]
            gh2_s[at, :] = jnp.zeros((chunk, width), F32)

        row_loop(rows, chunk, start)
        for i in range(rows // 128):
            h2t_s[:, i * 128 : (i + 1) * 128] = (
                h2_ref[i * 128 : (i + 1) * 128, :].astype(F32).T.astype(BF16)
            )

    dbu_ref[...] = jnp.zeros_like(dbu_ref)

    def middle(at):
        u = dot(h2_ref[at, :], wu_ref[...]) + bu_ref[...]
        phi, bell = gelu_parts(u)
        a = (u * phi).astype(BF16)
        a_s[at, :] = a
        ga = dot(gm_s[at, :], wd_ref[...], NT)
        gu = (ga * (phi + u * bell)).astype(BF16)
        gu_s[at, :] = gu
        dbu_ref[...] += factor * jnp.sum(gu.astype(F32), axis=0, keepdims=True)
        m_s[at, :] += dot(a, wd_ref[...])
        gh2_s[at, :] += dot(gu, wu_ref[...], NT)

    row_loop(rows, chunk // 2, middle)
    dwd_ref[...] = factor * lax.dot_general(
        a_s[...], gm_s[...], (((0,), (0,)), ((), ())), preferred_element_type=F32
    )
    dwu_ref[...] = factor * dot(h2t_s[...], gu_s[...])

    @pl.when(step == last)
    def _():
        def finish(at):
            out_ref[at, :] = m_s[at, :].astype(BF16)
            hat, rstd = row_stats(r_ref[at, :])
            gy = gh2_s[at, :]
            small_ref[1:2, :] += factor * jnp.sum(gy * hat, axis=0, keepdims=True)
            small_ref[2:3, :] += factor * jnp.sum(gy, axis=0, keepdims=True)
            gy = gy * g2_ref[...]
            first = jnp.mean(gy, axis=-1, keepdims=True)
            second = jnp.mean(gy * hat, axis=-1, keepdims=True)
            gr = gm_s[at, :].astype(F32) + rstd * (gy - first - hat * second)
            gr_ref[at, :] = gr
            gz = gr.astype(BF16)
            gm_s[at, :] = gz
            small_ref[3:4, :] += factor * jnp.sum(gz.astype(F32), axis=0, keepdims=True)
            go_ref[at, :] = dot(gz, wo_ref[...], NT).astype(BF16)

        row_loop(rows, chunk // 2, finish)
        dwo_ref[...] = factor * sum(
            dot(ot_ref[b], gm_s[b * span : (b + 1) * span, :]) for b in range(blocks)
        )


def backward_kernel(
    head_dim,
    blocks,
    factor_ref,
    x_ref,
    h1_ref,
    gr_ref,
    g1_ref,
    qg_ref,
    kg_ref,
    segc_ref,
    segr_ref,
    qn_ref,
    kn_ref,
    v_ref,
    go_ref,
    qhat_ref,
    khat_ref,
    qrstd_ref,
    krstd_ref,
    lse_ref,
    wq_ref,
    wk_ref,
    wv_ref,
    gx_ref,
    dw_ref,
    db_ref,
    small_ref,
    norm_ref,
    mask_s,
    h1t_s,
    kt_s,
    gqt_s,
    gq_s,
    gk_s,
    gv_s,
    g16_s,
    gh1_s,
):
    rows, width = x_ref.shape
    group = wq_ref.shape[1]
    heads = group // head_dim
    span = rows // blocks
    chunk = span // 2
    step = pl.program_id(0)
    last = pl.num_programs(0) - 1
    scale = jnp.asarray(head_dim**-0.5, BF16)
    factor = factor_ref[0]

    @pl.when(step == 0)
    def _():
        small_ref[...] = jnp.zeros_like(small_ref)
        norm_ref[...] = jnp.zeros_like(norm_ref)
        for b in range(blocks):
            same = segc_ref[b * span : (b + 1) * span, :] == segr_ref[b]
            mask_s[b] = jnp.where(same, OPEN, MASKED)
        for i in range(rows // 128):
            h1t_s[:, i * 128 : (i + 1) * 128] = (
                h1_ref[i * 128 : (i + 1) * 128, :].astype(F32).T.astype(BF16)
            )

        def zero(at):
            gh1_s[at, :] = jnp.zeros((chunk, width), F32)

        row_loop(rows, chunk, zero)

    def clear(at):
        gk_s[at, :] = jnp.zeros((chunk, group), F32)
        gv_s[at, :] = jnp.zeros((chunk, group), F32)

    row_loop(rows, chunk, clear)
    for b in range(blocks):
        kt_s[b] = (kn_ref[b * span : (b + 1) * span, :] * scale).astype(F32).T.astype(BF16)

    lane_head = lax.broadcasted_iota(jnp.int32, (span, group), 1) // head_dim

    def one(i, carry):
        h = i // blocks
        b = i % blocks
        at = pl.ds(pl.multiple_of(b * span, span), span)
        mine = lane_head == h

        def only(piece):
            return jnp.where(mine, piece, jnp.zeros_like(piece))

        queries = only(qn_ref[at, :] * scale)
        grads = only(go_ref[at, :])
        scores = jnp.minimum(dot(kn_ref[at, :], queries, NT), mask_s[b])
        probs = jnp.exp(scores - lse_ref[h, b])
        gprobs = dot(v_ref[at, :], grads, NT)
        inner = jnp.sum(probs * gprobs, axis=0, keepdims=True)
        gscores = (probs * (gprobs - inner)).astype(BF16)
        gv_s[at, :] += dot(probs.astype(BF16), grads)
        gk_s[at, :] += dot(gscores, queries)
        lanes = pl.ds(pl.multiple_of(h * head_dim, head_dim), head_dim)
        gqt_s[b, lanes, :] = dot(kt_s[b, lanes, :], gscores)
        return carry

    lax.fori_loop(0, heads * blocks, one, 0)
    for b in range(blocks):
        gq_s[b * span : (b + 1) * span, :] = gqt_s[b].T

    averager = averager_of(group, head_dim)

    def undo(at):
        def norm_back(g, hat_ref, rstd_ref, gain):
            hat = hat_ref[at, :]
            dgain = jnp.sum(g * hat, axis=0, keepdims=True)
            gy = g * gain
            first = head_mean(gy, averager)
            second = head_mean(gy * hat, averager)
            return rstd_ref[at, :] * (gy - first - hat * second), dgain

        gqn = gq_s[at, :]
        gq, dqg = norm_back(gqn, qhat_ref, qrstd_ref, qg_ref[...])
        norm_ref[0:1, :] += factor * dqg
        norm_ref[1:2, :] += factor * jnp.sum(gqn, axis=0, keepdims=True)
        gk, dkg = norm_back(gk_s[at, :], khat_ref, krstd_ref, kg_ref[...])
        norm_ref[2:3, :] += factor * dkg
        total = gh1_s[at, :]
        for j, (g, w_ref) in enumerate(((gq, wq_ref), (gk, wk_ref), (gv_s[at, :], wv_ref))):
            g16 = g.astype(BF16)
            g16_s[j, at, :] = g16
            total += dot(g16, w_ref[...], NT)
        gh1_s[at, :] = total

    row_loop(rows, chunk, undo)
    for j in range(3):
        g16 = g16_s[j]
        dw_ref[j] = factor * dot(h1t_s[...], g16)
        db_ref[j] = factor * jnp.sum(g16.astype(F32), axis=0, keepdims=True)

    @pl.when(step == last)
    def _():
        def finish(at):
            hat, rstd = row_stats(x_ref[at, :].astype(F32))
            gy = gh1_s[at, :]
            small_ref[0:1, :] += factor * jnp.sum(gy * hat, axis=0, keepdims=True)
            small_ref[1:2, :] += factor * jnp.sum(gy, axis=0, keepdims=True)
            gy = gy * g1_ref[...]
            first = jnp.mean(gy, axis=-1, keepdims=True)
            second = jnp.mean(gy * hat, axis=-1, keepdims=True)
            gx_ref[at, :] = (gr_ref[at, :] + rstd * (gy - first - hat * second)).astype(BF16)

        row_loop(rows, chunk // 2, finish)


def shape(dims, dtype):
    return jax.ShapeDtypeStruct(dims, dtype)


def whole(dims):
    return pl.BlockSpec(dims, lambda i: (0,) * len(dims))


def columns(rows, width, skip=0):
    return pl.BlockSpec((rows, width), lambda i: (0, i + skip))


SMEM = pl.BlockSpec(memory_space=pltpu.SMEM)
PARAMS = pltpu.CompilerParams(vmem_limit_bytes=VMEM)


def layer(
    tokens, ln1_gain, ln1_bias, w_qkv, b_qkv, qnorm_gain, qnorm_bias, knorm_gain, w_out, b_out,
    ln2_gain, ln2_bias, w_up, b_up, w_down, b_down, segment_ids, bucket_ids, share_counts, cotangent,
):
    rows, width = tokens.shape
    head_dim = qnorm_gain.shape[0]
    hidden = w_up.shape[1]
    blocks = 2
    span = rows // blocks
    group = min(GROUP, width)
    steps = width // group
    heads = group // head_dim

    def row(v):
        return v.astype(F32).reshape(1, -1)

    def tiled(v):
        return jnp.tile(row(v), (1, heads))

    counts = share_counts.astype(F32)
    share = jnp.sum(jnp.where(jnp.arange(2) == bucket_ids[0], counts, 0.0)) / jnp.sum(counts)
    total_slots = lax.axis_size("wide") * lax.axis_size("narrow") * rows
    factor = (share * lax.rsqrt(jnp.float32(total_slots))).reshape(1)
    segc = segment_ids.reshape(rows, 1)
    segr = segment_ids.reshape(blocks, 1, span)
    live = (segc >= 0).astype(F32)
    bias_qkv = row(b_qkv)
    q_gain, q_bias, k_gain = tiled(qnorm_gain), tiled(qnorm_bias), tiled(knorm_gain)

    by_group = columns(rows, group)
    lse_spec = pl.BlockSpec((heads, blocks, 1, span), lambda i: (i, 0, 0, 0))
    h1, qn, kn, v16, qhat, khat, qrstd, krstd, lse, o_t, resid, h2 = pl.pallas_call(
        functools.partial(forward_kernel, head_dim, blocks),
        grid=(steps,),
        in_specs=[
            SMEM,
            whole((rows, width)),
            whole((1, width)),
            whole((1, width)),
            columns(width, group),
            columns(width, group, steps),
            columns(width, group, 2 * steps),
            columns(1, group),
            columns(1, group, steps),
            columns(1, group, 2 * steps),
            whole((1, group)),
            whole((1, group)),
            whole((1, group)),
            pl.BlockSpec((group, width), lambda i: (i, 0)),
            whole((1, width)),
            whole((1, width)),
            whole((1, width)),
            whole((rows, 1)),
            whole((blocks, 1, span)),
        ],
        out_specs=[
            whole((rows, width)),
            by_group,
            by_group,
            by_group,
            by_group,
            by_group,
            by_group,
            by_group,
            lse_spec,
            pl.BlockSpec((blocks, group, span), lambda i: (0, i, 0)),
            whole((rows, width)),
            whole((rows, width)),
        ],
        out_shape=[
            shape((rows, width), BF16),
            shape((rows, width), BF16),
            shape((rows, width), BF16),
            shape((rows, width), BF16),
            shape((rows, width), F32),
            shape((rows, width), F32),
            shape((rows, width), F32),
            shape((rows, width), F32),
            shape((steps * heads, blocks, 1, span), F32),
            shape((blocks, width, span), BF16),
            shape((rows, width), F32),
            shape((rows, width), BF16),
        ],
        scratch_shapes=[
            pltpu.VMEM((blocks, blocks, span, span), F32),
            pltpu.VMEM((blocks, group, span), BF16),
            pltpu.VMEM((blocks, group, span), F32),
            pltpu.VMEM((rows, group), BF16),
        ],
        compiler_params=PARAMS,
        name="attention_forward",
    )(
        bucket_ids, tokens, row(ln1_gain), row(ln1_bias), w_qkv, w_qkv, w_qkv, bias_qkv, bias_qkv, bias_qkv,
        q_gain, q_bias, k_gain, w_out, row(b_out), row(ln2_gain), row(ln2_bias), segc, segr,
    )

    ff = min(768, hidden)
    out_tokens, grad_resid, go, d_w_down, d_w_up, d_w_out, d_b_up, small_two = pl.pallas_call(
        functools.partial(mlp_kernel, blocks),
        grid=(hidden // ff,),
        in_specs=[
            SMEM,
            whole((rows, width)),
            whole((rows, width)),
            whole((rows, width)),
            whole((rows, 1)),
            columns(width, ff),
            columns(1, ff),
            pl.BlockSpec((ff, width), lambda i: (i, 0)),
            whole((1, width)),
            whole((1, width)),
            whole((width, width)),
            whole((blocks, width, span)),
        ],
        out_specs=[
            whole((rows, width)),
            whole((rows, width)),
            whole((rows, width)),
            pl.BlockSpec((ff, width), lambda i: (i, 0)),
            columns(width, ff),
            whole((width, width)),
            columns(1, ff),
            whole((8, width)),
        ],
        out_shape=[
            shape((rows, width), BF16),
            shape((rows, width), F32),
            shape((rows, width), BF16),
            shape((hidden, width), F32),
            shape((width, hidden), F32),
            shape((width, width), F32),
            shape((1, hidden), F32),
            shape((8, width), F32),
        ],
        scratch_shapes=[
            pltpu.VMEM((rows, width), BF16),
            pltpu.VMEM((width, rows), BF16),
            pltpu.VMEM((rows, ff), BF16),
            pltpu.VMEM((rows, ff), BF16),
            pltpu.VMEM((rows, width), F32),
            pltpu.VMEM((rows, width), F32),
        ],
        compiler_params=PARAMS,
        name="mlp",
    )(
        factor, h2, resid, cotangent, live, w_up, row(b_up), w_down, row(b_down), row(ln2_gain), w_out, o_t,
    )

    grad_tokens, d_qkv, d_b_qkv, small_one, small_norm = pl.pallas_call(
        functools.partial(backward_kernel, head_dim, blocks),
        grid=(steps,),
        in_specs=[
            SMEM,
            whole((rows, width)),
            whole((rows, width)),
            whole((rows, width)),
            whole((1, width)),
            whole((1, group)),
            whole((1, group)),
            whole((rows, 1)),
            whole((blocks, 1, span)),
            by_group,
            by_group,
            by_group,
            by_group,
            by_group,
            by_group,
            by_group,
            by_group,
            lse_spec,
            columns(width, group),
            columns(width, group, steps),
            columns(width, group, 2 * steps),
        ],
        out_specs=[
            whole((rows, width)),
            pl.BlockSpec((3, width, group), lambda i: (0, 0, i)),
            pl.BlockSpec((3, 1, group), lambda i: (0, 0, i)),
            whole((8, width)),
            whole((8, group)),
        ],
        out_shape=[
            shape((rows, width), BF16),
            shape((3, width, width), F32),
            shape((3, 1, width), F32),
            shape((8, width), F32),
            shape((8, group), F32),
        ],
        scratch_shapes=[
            pltpu.VMEM((blocks, span, span), F32),
            pltpu.VMEM((width, rows), BF16),
            pltpu.VMEM((blocks, group, span), BF16),
            pltpu.VMEM((blocks, group, span), F32),
            pltpu.VMEM((rows, group), F32),
            pltpu.VMEM((rows, group), F32),
            pltpu.VMEM((rows, group), F32),
            pltpu.VMEM((3, rows, group), BF16),
            pltpu.VMEM((rows, width), F32),
        ],
        compiler_params=PARAMS,
        name="attention_backward",
    )(
        factor, tokens, h1, grad_resid, row(ln1_gain), q_gain, k_gain, segc, segr, qn, kn, v16, go,
        qhat, khat, qrstd, krstd, lse, w_qkv, w_qkv, w_qkv,
    )
    return out_tokens, grad_tokens, d_w_down, d_w_up, d_w_out, d_qkv, d_b_up, small_two, d_b_qkv, small_one, small_norm


def on_device(*args):
    width = args[0].shape[1]
    head_dim = args[5].shape[0]
    (out_tokens, grad_tokens, d_w_down, d_w_up, d_w_out, d_qkv, d_b_up, small_two, d_b_qkv, small_one, small_norm) = layer(*args)
    both = ("wide", "narrow")
    d_w_down, d_w_up, d_w_out = lax.psum((d_w_down, d_w_up, d_w_out), both)
    small = jnp.concatenate(
        [
            small_one[:2].reshape(-1),
            d_b_qkv.reshape(-1),
            small_norm[:3].reshape(3, -1, head_dim).sum(axis=1).reshape(-1),
            small_two[:4].reshape(-1),
            d_b_up.reshape(-1),
        ]
    )
    d_qkv, small = lax.psum((d_qkv, small), both)
    d_w_qkv = jnp.transpose(d_qkv, (1, 0, 2)).reshape(width, -1)
    sizes = (width, width, 3 * width, head_dim, head_dim, head_dim, width, width, width, width, d_b_up.size)
    parts, at = [], 0
    for size in sizes:
        parts.append(small[at : at + size])
        at += size
    d_g1, d_b1, d_bqkv, d_qg, d_qb, d_kg, d_bd, d_g2, d_b2, d_bo, d_bu = parts
    return (
        out_tokens, grad_tokens, d_g1, d_b1, d_w_qkv, d_bqkv, d_qg, d_qb, d_kg, d_w_out, d_bo,
        d_g2, d_b2, d_w_up, d_bu, d_w_down, d_bd,
    )


def solution(mesh):
    rows = P(("wide", "narrow"), None)
    in_specs = (rows,) + (P(),) * 15 + (P(("wide", "narrow")), P("wide"), P(), rows)
    out_specs = (rows, rows) + (P(),) * 15
    return jax.shard_map(
        on_device, mesh=mesh, in_specs=in_specs, out_specs=out_specs, check_vma=False
    )
```
